32 devices in a mesh: groups: 2 (over x), expert: 16 (over z, y, core).
Axes of the slice: x: 2, y: 2, z: 4, core: 2. Of those that a mesh axis runs over, the one named last changes fastest.
Arguments:
- queries: bfloat16 [1024, 4096], P(('groups', 'expert')), parts along dimension 0, may hold values from -6 to 6
- incoming_key_value: bfloat16 [1024, 512], P(('groups', 'expert')), parts along dimension 0, may hold values from -6 to 6
- key_value_codes: bfloat16 [4096, 16, 512], P(('groups', 'expert')), parts along dimension 0, may hold values from -6 to 6
- key_value_scales: bfloat16 [4096, 4, 16], P(('groups', 'expert')), parts along dimension 0, may hold values from 0.25 to 96
- lengths: int32 [32, 32], P(('groups', 'expert')), parts along dimension 0, may hold values from 1 to 64, 1024 in all within a row
- block_table: int32 [32, 32, 4], P(('groups', 'expert')), parts along dimension 0, may hold values from 0 to 127, as said below
- hidden: bfloat16 [1024, 2048], P(('groups', 'expert')), parts along dimension 0, may hold values from -6 to 6
- routes: int32 [1024, 8], P(('groups', 'expert')), parts along dimension 0, may hold values from 0 to 15, all different within a row; in each aligned block of 32 rows (0 to 31, 32 to 63, ...) at most 32 rows name the same one
- router: bfloat16 [2048, 16], replicated, may hold values from -0.125 to 0.125
- w_gate: bfloat16 [16, 2048, 768], P('expert'), may hold values from -0.125 to 0.125
- w_up: bfloat16 [16, 2048, 768], P('expert'), may hold values from -0.125 to 0.125
- w_down: bfloat16 [16, 768, 2048], P('expert'), may hold values from -0.21875 to 0.21875
Outputs:
- attn_out: bfloat16 [1024, 4096], P(('groups', 'expert')), parts along dimension 0
- moe_out: bfloat16 [1024, 2048], P(('groups', 'expert')), parts along dimension 0
The draws below stay inside these ranges and needn't reach their ends.
There are 2 independent parts, one for each index of `groups`. The reference program is written for one: setup_inputs(seed, part) draws one part's arguments, and reference() takes and returns one part's arrays. A program takes and returns all parts, laid end to end along the dimension named above; an argument that names none is the same for every part. Nothing has to cross between parts.
Inputs may be any that keep to these rules, and one draw needn't show every extreme that they name: The 32 lengths of one device sum to 1024, and one of them equals 64. `block_table`: on each device the 32 x 4 entries name each of the 128 pool slots exactly once. `routes`: each row names 8 different experts; at most 32 rows of one device name the same expert, and exactly 32 do for some expert and device.
All inputs are finite; a program needn't handle non-finite values.
Results may differ from the reference program's by a relative error of at most 0.0085.
Values may be sent and summed in bfloat16 or wider, within the bound.
A program may use at most 64 MiB of HBM per device.

```python
import math
import jax
import jax.numpy as jnp
import numpy as np
from jax import lax

D = 2048
FF = 768
QUERY_HEADS = 32
KEY_VALUE_HEADS = 2
HEAD_SIZE = 128
TOPK = 8
BLOCK_TOKENS = 16
ROWS = 32
PROMPT_MAXIMUM = 64
REQUEST_BLOCKS = 4
DEVICE_BLOCKS = 128
PEER_BLOCKS = 8
EXPERTS = 16
MOST = 32
DECODE_REQUESTS = 512
N_EXPERT = 16


def draw_block_table(key, part):
    key = jax.random.fold_in(key, 5)
    subkeys = jax.random.split(key, N_EXPERT)
    orders = jax.vmap(lambda single: jax.random.permutation(single, DEVICE_BLOCKS))(subkeys)
    return orders.reshape(N_EXPERT, ROWS, REQUEST_BLOCKS).astype(jnp.int32)


def draw_key_value_scales(key, part):
    key = jax.random.fold_in(key, 9)
    draw_one = jax.random.fold_in(key, 0)
    extent_length = (N_EXPERT * DEVICE_BLOCKS, 2 * KEY_VALUE_HEADS, BLOCK_TOKENS)
    values = jnp.exp(jax.random.uniform(draw_one, extent_length, jnp.float32, math.log(0.25), 0.0))
    return values.astype(jnp.bfloat16)


def block_scale(key, extent, shards, smallest, high):
    factor_of, own = 1.0, jax.random.fold_in(key, 6)
    for position, blocks in shards:
        heights = jnp.exp(jax.random.uniform(jax.random.fold_in(own, position), (blocks,), jnp.float32, smallest / len(shards), high / len(shards)))
        factor_of = factor_of * jnp.repeat(heights, extent[position] // blocks).reshape([-1 if axis == position else 1 for axis in range(len(extent))])
    return factor_of


def split_up(amount, total, reach, skew):
    portions = [(1 << 20) // math.isqrt(grade ** skew) + 1 for grade in range(2, amount + 1)]
    rest, holding = total - reach - (amount - 1), [1] * (amount - 1)
    while rest > 0:
        movable = [i for i in range(amount - 1) if holding[i] < reach]
        mass, remaining = sum([portions[i] for i in movable]), rest
        for i in movable:
            addition = min(reach - holding[i], max(1, remaining * portions[i] // mass), rest)
            holding[i] = holding[i] + addition
            rest = rest - addition
    return np.array([reach] + holding)


def ragged(own_key, count, total, most, slope):
    if count == 2:
        one = jax.random.randint(own_key, (), max(1, total - most), min(most, total - 1) + 1)
        return jnp.stack([one, total - one])
    sizes = jnp.asarray(split_up(count, total, most, slope), jnp.int32)
    pairs = (count - 1) // 2
    giver, sink = sizes[1:1 + 2 * pairs:2], sizes[2:2 + 2 * pairs:2]
    margin = jnp.minimum(giver - 1, most - sink)
    passed = jax.random.randint(jax.random.fold_in(own_key, 1), (pairs,), 0, 1 << 20) % (margin + 1)
    sizes = sizes.at[1:1 + 2 * pairs:2].set(giver - passed).at[2:2 + 2 * pairs:2].set(sink + passed)
    return sizes[jax.random.permutation(jax.random.fold_in(own_key, 2), count)]


def routed_block(key, own, number, rows, number_of, top, reach, skew):
    ranking = jax.random.permutation(key, number_of)
    crowded, common = shares(number_of, rows * top, reach, skew, True), shares(number_of, rows * top, reach, skew, False)
    places = jnp.arange(number_of)

    def named(sizes, offset_by):
        used = int((sizes > 0).sum())
        fixed = max(1, used // 4)
        shifted = fixed + (places - fixed + offset_by * (used - fixed)) % max(1, number_of - fixed)
        return jnp.zeros((number_of,), jnp.int32).at[ranking[jnp.where(places < fixed, places, shifted)]].set(jnp.asarray(sizes, jnp.int32))

    sizes = jnp.where(number % 4 == 0, named(crowded, number // 4), named(common, number - number // 4 - 1))
    mixed = jax.random.permutation(jax.random.fold_in(own, 3), number_of)
    giver, taker = mixed[0:number_of // 2 * 2:2], mixed[1:number_of // 2 * 2:2]
    room = jnp.minimum(sizes[giver] - 1, reach - sizes[taker]) // 2
    room = jnp.where((giver == ranking[0]) | (taker == ranking[0]) | (sizes[taker] == 0), 0, jnp.maximum(room, 0))
    shifted = jax.random.randint(jax.random.fold_in(own, 4), (number_of // 2,), 0, 1 << 20) % (room + 1)
    sizes = sizes.at[giver].add(-shifted).at[taker].add(shifted)
    items = jnp.searchsorted(jnp.cumsum(sizes), jnp.arange(rows * top), side="right").astype(jnp.int32)
    table = items.reshape(top, rows).T
    table = table[jax.random.permutation(jax.random.fold_in(own, 1), rows)]
    offset_by = jax.random.randint(jax.random.fold_in(own, 2), (rows, 1), 0, top)
    return jnp.take_along_axis(table, (jnp.arange(top)[None, :] + offset_by) % top, axis=1)


def shares(amount, total, bound, slope, full):
    weights = [(1 << 20) // math.isqrt(grade ** slope) + 1 for grade in range(1, amount + 1)]
    largest = bound if full else min(bound, max(-(-total // amount), total * weights[0] // sum(weights)))
    least = 1 if total - largest >= amount - 1 else 0
    holding, surplus = [largest] + [least] * (amount - 1), total - largest - least * (amount - 1)
    while surplus > 0:
        candidates = [i for i in range(1, amount) if holding[i] < largest] or [i for i in range(1, amount) if holding[i] < bound]
        whole, left = sum([weights[i] for i in candidates]), surplus
        for i in candidates:
            extra = min(bound - holding[i], max(1, left * weights[i] // whole), surplus)
            holding[i] = holding[i] + extra
            surplus = surplus - extra
    return np.array(holding)


def scatter_about(own_key, dims, scale, bound, cuts=(), kind=jnp.bfloat16):
    result = jax.random.normal(own_key, dims, jnp.float32) * scale
    if len(cuts) > 0:
        result = block_scale(own_key, dims, cuts, -0.22, 0.18) * result
    return jnp.clip(result, min=-bound, max=bound).astype(kind)


def setup_inputs(seed: int = 0, part: int = 0) -> dict:
    keys = jax.random.split(jax.random.key(seed), 13)
    own_keys = jax.random.split(jax.random.fold_in(keys[12], part), 13)
    queries = scatter_about(own_keys[0], (DECODE_REQUESTS, QUERY_HEADS * HEAD_SIZE), 1.0, 6.0, ((0, 16),))
    incoming_key_value = scatter_about(own_keys[1], (DECODE_REQUESTS, 2 * KEY_VALUE_HEADS * HEAD_SIZE), 1.0, 6.0, ((0, 16),))
    key_value_codes = scatter_about(own_keys[2], (N_EXPERT * DEVICE_BLOCKS, BLOCK_TOKENS, 2 * KEY_VALUE_HEADS * HEAD_SIZE), 1.0, 6.0, ((0, 16),))
    key_value_scales = draw_key_value_scales(jax.random.fold_in(jax.random.fold_in(keys[12], part), 71), part)
    lengths = jax.vmap(lambda own: ragged(own, ROWS, ROWS * PROMPT_MAXIMUM // 2, PROMPT_MAXIMUM, 2))(jax.random.split(own_keys[4], N_EXPERT)).reshape((N_EXPERT, ROWS)).astype(jnp.int32)
    block_table = draw_block_table(jax.random.fold_in(jax.random.fold_in(keys[12], part), 71), part)
    hidden = scatter_about(own_keys[6], (DECODE_REQUESTS, D), 1.0, 6.0, ((0, 16),))
    routes_keys = jax.random.split(jax.random.fold_in(own_keys[7], 1), DECODE_REQUESTS // ROWS)
    routes_turns = jax.random.permutation(jax.random.fold_in(own_keys[7], 3), DECODE_REQUESTS // ROWS)
    routes = jax.vmap(lambda own, number: routed_block(jax.random.fold_in(own_keys[7], 2), own, number, ROWS, EXPERTS, TOPK, MOST, 2))(routes_keys, routes_turns).reshape((DECODE_REQUESTS, TOPK))
    router = scatter_about(keys[8], (D, EXPERTS), D ** -0.5, 0.125)
    w_gate = scatter_about(keys[9], (EXPERTS, D, FF), D ** -0.5, 0.125, ((0, 16),))
    w_up = scatter_about(keys[10], (EXPERTS, D, FF), D ** -0.5, 0.125, ((0, 16),))
    w_down = scatter_about(keys[11], (EXPERTS, FF, D), FF ** -0.5, 0.21875, ((0, 16),))
    return {"queries": queries, "incoming_key_value": incoming_key_value, "key_value_codes": key_value_codes, "key_value_scales": key_value_scales, "lengths": lengths, "block_table": block_table, "hidden": hidden, "routes": routes, "router": router, "w_gate": w_gate, "w_up": w_up, "w_down": w_down}


def attend_rows(query_row_block, newest_key_value, device_block_codes, device_block_scales, prompt_lens, block_row_slice):
    count_of_rows = query_row_block.shape[0]
    head_groups = QUERY_HEADS // KEY_VALUE_HEADS
    inv_root = 1.0 / math.sqrt(HEAD_SIZE)
    cached_entries = device_block_codes[block_row_slice].reshape(count_of_rows, PROMPT_MAXIMUM, 2, KEY_VALUE_HEADS, HEAD_SIZE)
    scale_values = device_block_scales[block_row_slice].reshape(count_of_rows, REQUEST_BLOCKS, 2, KEY_VALUE_HEADS, BLOCK_TOKENS)
    scale_values = jnp.transpose(scale_values, (0, 2, 3, 1, 4)).reshape(count_of_rows, 2, KEY_VALUE_HEADS, PROMPT_MAXIMUM).astype(jnp.float32)
    query_head_count = query_row_block.reshape(count_of_rows, KEY_VALUE_HEADS, head_groups, HEAD_SIZE).astype(jnp.float32)
    key_codes = cached_entries[:, :, 0].astype(jnp.float32)
    value_codes = cached_entries[:, :, 1].astype(jnp.float32)
    raw_dots = jnp.einsum('rhgd,rthd->rhgt', query_head_count, key_codes)
    scores = raw_dots * scale_values[:, 0][:, :, None, :] * inv_root
    newest_key = newest_key_value[:, :KEY_VALUE_HEADS * HEAD_SIZE].reshape(count_of_rows, KEY_VALUE_HEADS, HEAD_SIZE).astype(jnp.float32)
    newest_value = newest_key_value[:, KEY_VALUE_HEADS * HEAD_SIZE:].reshape(count_of_rows, KEY_VALUE_HEADS, HEAD_SIZE).astype(jnp.float32)
    own_score = jnp.einsum('rhgd,rhd->rhg', query_head_count, newest_key) * inv_root
    live_mask = (jnp.arange(PROMPT_MAXIMUM, dtype=jnp.int32)[None, :] < prompt_lens[:, None])[:, None, None, :]
    masked = jnp.where(live_mask, scores, -1e+30)
    peak_score = jnp.maximum(lax.optimization_barrier(jnp.max(masked, axis=-1)), own_score)
    exp_terms = jnp.where(live_mask, jnp.exp(masked - peak_score[..., None]), 0.0)
    own_exp = jnp.exp(own_score - peak_score)
    totals = lax.optimization_barrier(jnp.sum(exp_terms, axis=-1)) + own_exp
    weights = (exp_terms / totals[..., None] * scale_values[:, 1][:, :, None, :]).astype(jnp.bfloat16)
    own_weight = (own_exp / totals).astype(jnp.bfloat16)
    mixture = jnp.einsum('rhgt,rthd->rhgd', weights.astype(jnp.float32), value_codes)
    mixture = mixture + own_weight.astype(jnp.float32)[..., None] * newest_value[:, :, None, :]
    return mixture.reshape(count_of_rows, QUERY_HEADS * HEAD_SIZE).astype(jnp.bfloat16)

def reference(queries, incoming_key_value, key_value_codes, key_value_scales, lengths, block_table, hidden, routes, router, w_gate, w_up, w_down):
    every_code = key_value_codes.reshape(N_EXPERT, N_EXPERT, PEER_BLOCKS, BLOCK_TOKENS, 2 * KEY_VALUE_HEADS * HEAD_SIZE)
    every_scale = key_value_scales.reshape(N_EXPERT, N_EXPERT, PEER_BLOCKS, 2 * KEY_VALUE_HEADS, BLOCK_TOKENS)

    def attend_device(device_number):
        device_block_codes = lax.dynamic_index_in_dim(every_code, device_number, 1, keepdims=False).reshape(DEVICE_BLOCKS, BLOCK_TOKENS, 2 * KEY_VALUE_HEADS * HEAD_SIZE)
        device_block_scales = lax.dynamic_index_in_dim(every_scale, device_number, 1, keepdims=False).reshape(DEVICE_BLOCKS, 2 * KEY_VALUE_HEADS, BLOCK_TOKENS)
        block_row_slice = lax.dynamic_index_in_dim(block_table, device_number, 0, keepdims=False)
        prompt_lens = lax.dynamic_index_in_dim(lengths, device_number, 0, keepdims=False)
        query_row_block = lax.dynamic_slice_in_dim(queries, device_number * ROWS, ROWS, 0)
        newest_key_value = lax.dynamic_slice_in_dim(incoming_key_value, device_number * ROWS, ROWS, 0)
        return attend_rows(query_row_block, newest_key_value, device_block_codes, device_block_scales, prompt_lens, block_row_slice)
    attn_out = lax.map(attend_device, jnp.arange(N_EXPERT, dtype=jnp.int32)).reshape(N_EXPERT * ROWS, QUERY_HEADS * HEAD_SIZE)
    flat_routes = routes.reshape(N_EXPERT, ROWS * TOPK)
    expert_hits = (flat_routes[:, :, None] == jnp.arange(EXPERTS, dtype=jnp.int32)[None, None, :]).astype(jnp.int32)
    before = jnp.cumsum(expert_hits, axis=1) - expert_hits
    slot_rank = lax.optimization_barrier(jnp.sum(before * expert_hits, axis=2))
    sources = jnp.arange(N_EXPERT, dtype=jnp.int32)[:, None]
    slot_index = sources * MOST + slot_rank
    global_row = sources * ROWS + jnp.arange(ROWS * TOPK, dtype=jnp.int32)[None, :] // TOPK
    row_table = jnp.full((EXPERTS, N_EXPERT * MOST), -1, dtype=jnp.int32)
    row_table = row_table.at[flat_routes.reshape(-1), slot_index.reshape(-1)].set(global_row.reshape(-1))

    def run_expert(expert_index):
        slot_rows = lax.dynamic_index_in_dim(row_table, expert_index, 0, keepdims=False)
        taken = hidden[jnp.maximum(slot_rows, 0)]
        gate_part = jnp.dot(taken, lax.dynamic_index_in_dim(w_gate, expert_index, 0, keepdims=False), preferred_element_type=jnp.float32)
        up_part = jnp.dot(taken, lax.dynamic_index_in_dim(w_up, expert_index, 0, keepdims=False), preferred_element_type=jnp.float32)
        inner_act = (jax.nn.silu(gate_part) * up_part).astype(jnp.bfloat16)
        return jnp.dot(inner_act, lax.dynamic_index_in_dim(w_down, expert_index, 0, keepdims=False), preferred_element_type=jnp.float32).astype(jnp.bfloat16)
    outputs = lax.map(run_expert, jnp.arange(EXPERTS, dtype=jnp.int32))
    picked = outputs[flat_routes.reshape(-1), slot_index.reshape(-1)].reshape(N_EXPERT * ROWS, TOPK, D)
    logits = jnp.dot(hidden, router, preferred_element_type=jnp.float32)
    chosen = jnp.take_along_axis(logits, routes, axis=1)
    gate_probs = jax.nn.softmax(chosen, axis=-1).astype(jnp.bfloat16)
    moe_out = lax.optimization_barrier(jnp.sum(gate_probs.astype(jnp.float32)[:, :, None] * picked.astype(jnp.float32), axis=1)).astype(jnp.bfloat16)
    return (attn_out, moe_out)
```

```python
import functools
import math

import jax
import jax.numpy as jnp
from jax import lax
from jax.experimental import pallas as pl
from jax.experimental.pallas import tpu as pltpu
from jax.sharding import PartitionSpec as P

QUERY_HEADS = 32
KEY_VALUE_HEADS = 2
HEAD_SIZE = 128


def attend(
    query_row_block,
    newest_key_value,
    device_block_codes,
    device_block_scales,
    prompt_lens,
    block_row_slice,
):
    count_of_rows = query_row_block.shape[0]
    block_list = block_row_slice.shape[1]
    block_length = device_block_codes.shape[1]
    context_tokens = block_list * block_length
    head_groups = QUERY_HEADS // KEY_VALUE_HEADS
    inv_root = 1.0 / math.sqrt(HEAD_SIZE)
    cached_entries = device_block_codes[block_row_slice].reshape(
        count_of_rows, context_tokens, 2, KEY_VALUE_HEADS, HEAD_SIZE
    )
    scale_values = device_block_scales[block_row_slice].reshape(
        count_of_rows, block_list, 2, KEY_VALUE_HEADS, block_length
    )
    scale_values = (
        jnp.transpose(scale_values, (0, 2, 3, 1, 4))
        .reshape(count_of_rows, 2, KEY_VALUE_HEADS, context_tokens)
        .astype(jnp.float32)
    )
    query_head_count = query_row_block.reshape(
        count_of_rows, KEY_VALUE_HEADS, head_groups, HEAD_SIZE
    )
    key_codes = cached_entries[:, :, 0]
    value_codes = cached_entries[:, :, 1]
    raw_dots = jnp.einsum(
        "rhgd,rthd->rhgt", query_head_count, key_codes, preferred_element_type=jnp.float32
    )
    scores = raw_dots * scale_values[:, 0][:, :, None, :] * inv_root
    newest_key = newest_key_value[:, : KEY_VALUE_HEADS * HEAD_SIZE].reshape(
        count_of_rows, KEY_VALUE_HEADS, HEAD_SIZE
    )
    newest_value = (
        newest_key_value[:, KEY_VALUE_HEADS * HEAD_SIZE :]
        .reshape(count_of_rows, KEY_VALUE_HEADS, HEAD_SIZE)
        .astype(jnp.float32)
    )
    own_score = (
        jnp.einsum(
            "rhgd,rhd->rhg", query_head_count, newest_key, preferred_element_type=jnp.float32
        )
        * inv_root
    )
    live_mask = (jnp.arange(context_tokens, dtype=jnp.int32)[None, :] < prompt_lens[:, None])[
        :, None, None, :
    ]
    masked = jnp.where(live_mask, scores, -1e30)
    peak_score = jnp.maximum(jnp.max(masked, axis=-1), own_score)
    exp_terms = jnp.where(live_mask, jnp.exp(masked - peak_score[..., None]), 0.0)
    own_exp = jnp.exp(own_score - peak_score)
    totals = jnp.sum(exp_terms, axis=-1) + own_exp
    weights = (exp_terms / totals[..., None] * scale_values[:, 1][:, :, None, :]).astype(
        jnp.bfloat16
    )
    own_weight = (own_exp / totals).astype(jnp.bfloat16)
    mixture = jnp.einsum(
        "rhgt,rthd->rhgd", weights, value_codes, preferred_element_type=jnp.float32
    )
    mixture = mixture + own_weight.astype(jnp.float32)[..., None] * newest_value[:, :, None, :]
    return mixture.reshape(count_of_rows, QUERY_HEADS * HEAD_SIZE).astype(jnp.bfloat16)


def local(
    queries,
    incoming_key_value,
    key_value_codes,
    key_value_scales,
    lengths,
    block_table,
    hidden,
    routes,
    router,
    w_gate,
    w_up,
    w_down,
):
    count_of_rows = hidden.shape[0]
    top_count = routes.shape[1]
    experts = router.shape[1]
    capacity = 2 * count_of_rows * top_count // experts
    flat_routes = routes.reshape(count_of_rows * top_count)
    columns = jnp.arange(experts, dtype=jnp.int32)
    expert_hits = (flat_routes[:, None] == columns[None, :]).astype(jnp.int32)
    slot_rank = jnp.sum((jnp.cumsum(expert_hits, axis=0) - expert_hits) * expert_hits, axis=1)
    slot_index = flat_routes * capacity + slot_rank
    slot_hot = (
        slot_index[:, None] == jnp.arange(experts * capacity, dtype=jnp.int32)[None, :]
    ).reshape(count_of_rows, top_count, experts * capacity)
    logits = jnp.dot(hidden, router, preferred_element_type=jnp.float32)
    chosen = jnp.sum(
        jnp.where(routes[:, :, None] == columns[None, None, :], logits[:, None, :], 0.0), axis=2
    )
    gate_probs = jax.nn.softmax(chosen, axis=-1).astype(jnp.bfloat16)
    device_block_codes, device_block_scales = (
        lax.all_to_all(key_value_codes, "expert", split_axis=0, concat_axis=0, tiled=True),
        lax.all_to_all(key_value_scales, "expert", split_axis=0, concat_axis=0, tiled=True),
    )
    dispatch_matrix = jnp.any(slot_hot, axis=1).astype(jnp.bfloat16)
    outgoing = jnp.einsum(
        "rs,rd->sd", dispatch_matrix, hidden, preferred_element_type=jnp.float32
    ).astype(jnp.bfloat16)
    received = lax.all_to_all(outgoing, "expert", split_axis=0, concat_axis=0, tiled=True)
    gate_part = jnp.dot(received, w_gate[0], preferred_element_type=jnp.float32)
    up_part = jnp.dot(received, w_up[0], preferred_element_type=jnp.float32)
    inner_act = (jax.nn.silu(gate_part) * up_part).astype(jnp.bfloat16)
    results = jnp.dot(inner_act, w_down[0], preferred_element_type=jnp.float32).astype(jnp.bfloat16)
    returned = lax.all_to_all(results, "expert", split_axis=0, concat_axis=0, tiled=True)
    combine_weights = jnp.sum(
        jnp.where(slot_hot, gate_probs.astype(jnp.float32)[:, :, None], 0.0), axis=1
    ).astype(jnp.bfloat16)
    moe_out = jnp.dot(combine_weights, returned, preferred_element_type=jnp.float32).astype(
        jnp.bfloat16
    )
    attn_out = attend(
        queries,
        incoming_key_value,
        device_block_codes,
        device_block_scales,
        lengths[0],
        block_table[0],
    )
    return (attn_out, moe_out)


MESH = pl.DeviceIdType.MESH
F32 = jnp.float32
BF16 = jnp.bfloat16


def fused_kernel(
    n,
    q_ref,
    new_ref,
    kv_ref,
    scale_ref,
    meta_ref,
    hid_ref,
    routes_ref,
    router_ref,
    wg_hbm,
    wu_hbm,
    wd_hbm,
    attn_ref,
    moe_ref,
    x,
    pool,
    scales,
    wg,
    wu,
    wd,
    act,
    part,
    r1,
    r2,
    r3,
    qh,
    m_ref,
    l_ref,
    acc,
    w_sem,
    own_sem,
    ag_s,
    ag_r,
    kv_s,
    kv_r,
    sc_s,
    sc_r,
    rs_s,
    rs_r,
):
    rows, width = hid_ref.shape
    ff = wg.shape[1]
    experts = router_ref.shape[1]
    depth = n // 4
    chips = n // 2
    heads = KEY_VALUE_HEADS
    group = QUERY_HEADS // heads
    tokens = pool.shape[1]
    me = lax.axis_index("expert")
    z, y, c = me // 4, (me // 2) % 2, me % 2
    chip = me // 2
    sibling = chip * 2 + (1 - c)

    def at(zz, yy, cc):
        return zz * 4 + yy * 2 + cc

    weights = [
        pltpu.make_async_copy(s, d, w_sem.at[i])
        for i, (s, d) in enumerate(((wg_hbm, wg), (wu_hbm, wu), (wd_hbm, wd)))
    ]
    for w in weights:
        w.start()
    own_kv = pltpu.make_async_copy(kv_ref.at[me], pool.at[me], own_sem.at[0])
    own_kv.start()

    barrier = pltpu.get_barrier_semaphore()
    for k in range(1, n):
        pl.semaphore_signal(
            barrier, inc=1, device_id={"expert": (me + k) % n}, device_id_type=MESH
        )

    logits = jnp.dot(hid_ref[...], router_ref[...], preferred_element_type=F32)
    lane = lax.broadcasted_iota(jnp.int32, (rows, experts), 1)
    chosen = lane < 0
    for k in range(routes_ref.shape[1]):
        chosen = jnp.logical_or(chosen, routes_ref[:, k : k + 1] == lane)
    logits = jnp.where(chosen, logits, -1e30)
    terms = jnp.where(chosen, jnp.exp(logits - jnp.max(logits, axis=1, keepdims=True)), 0.0)
    gates = (terms / jnp.sum(terms, axis=1, keepdims=True)).astype(BF16)
    spread = (
        lax.broadcasted_iota(jnp.int32, (experts, 128), 0)
        == lax.broadcasted_iota(jnp.int32, (experts, 128), 1)
    ).astype(BF16)
    x[me, :, :width] = hid_ref[...]
    x[me, :, width:] = jnp.dot(gates, spread, preferred_element_type=F32).astype(BF16)
    scales[me] = scale_ref[me]

    pl.semaphore_wait(barrier, n - 1)

    def ag(src, slot, target):
        return pltpu.make_async_remote_copy(
            src_ref=x.at[src],
            dst_ref=x.at[src],
            send_sem=ag_s.at[slot],
            recv_sem=ag_r.at[src],
            device_id={"expert": target},
            device_id_type=MESH,
        )

    def kv(dest, source):
        return pltpu.make_async_remote_copy(
            src_ref=kv_ref.at[dest],
            dst_ref=pool.at[source],
            send_sem=kv_s.at[dest],
            recv_sem=kv_r.at[source],
            device_id={"expert": dest},
            device_id_type=MESH,
        )

    def sc(dest, source):
        return pltpu.make_async_remote_copy(
            src_ref=scale_ref.at[dest],
            dst_ref=scales.at[source],
            send_sem=sc_s.at[dest],
            recv_sem=sc_r.at[source],
            device_id={"expert": dest},
            device_id_type=MESH,
        )

    for d in range(1, depth):
        ag(me, d - 1, at((z + d) % depth, y, c)).start()
    ag(me, depth - 1, at(z, 1 - y, c)).start()
    ag(me, 2 * depth - 1, sibling).start()

    kv_order = [sibling]
    for j in range(1, chips):
        for cc in range(2):
            kv_order.append(((chip + j) % chips) * 2 + (c + cc) % 2)
    for dest in kv_order:
        sc(dest, me).start()
        kv(dest, me).start()

    req_of_row = lax.broadcasted_iota(jnp.int32, (group * rows, 1), 0) % rows
    for h in range(heads):
        for g in range(group):
            at_lane = (h * group + g) * HEAD_SIZE
            qh[h, g * rows : (g + 1) * rows, :] = q_ref[:, at_lane : at_lane + HEAD_SIZE]
        k_new = new_ref[:, h * HEAD_SIZE : (h + 1) * HEAD_SIZE].astype(F32)
        v_new = new_ref[:, (heads + h) * HEAD_SIZE : (heads + h + 1) * HEAD_SIZE].astype(F32)
        for g in range(group):
            own = jnp.sum(
                qh[h, g * rows : (g + 1) * rows, :].astype(F32) * k_new, axis=1, keepdims=True
            ) * (1.0 / math.sqrt(HEAD_SIZE))
            m_ref[h, g * rows : (g + 1) * rows, :] = jnp.broadcast_to(own, (rows, HEAD_SIZE))
            acc[h, g * rows : (g + 1) * rows, :] = v_new
        first = lax.broadcasted_iota(jnp.int32, (group * rows, HEAD_SIZE), 1) == 0
        l_ref[h] = jnp.where(first, 1.0, 0.0)

    for d in range(1, depth):
        src = at((z + depth - d) % depth, y, c)
        ag(src, 0, sibling).wait_recv()
        ag(src, depth - 1 + d, at(z, 1 - y, c)).start()
        ag(src, 2 * depth - 1 + d, sibling).start()
    for d in range(depth):
        src = at((z + depth - d) % depth, 1 - y, c)
        ag(src, 0, sibling).wait_recv()
        ag(src, 3 * depth - 1 + d, sibling).start()
    for zz in range(depth):
        for yy in range(2):
            ag(at(zz, yy, 1 - c), 0, sibling).wait_recv()

    weights[0].wait()
    weights[1].wait()
    tile = 256

    def up_body(t, _):
        cols = pl.ds(pl.multiple_of(t * tile, tile), tile)
        xs = x[:, :, :width].reshape(n * rows, width)
        g = jnp.dot(xs, wg[:, cols], preferred_element_type=F32)
        u = jnp.dot(xs, wu[:, cols], preferred_element_type=F32)
        act[:, cols] = (g / (1.0 + jnp.exp(-g)) * u).astype(BF16)
        return 0

    lax.fori_loop(0, ff // tile, up_body, 0)
    weights[2].wait()
    all_gates = x[:, :, width:].reshape(n * rows, 128).astype(F32)
    here = lax.broadcasted_iota(jnp.int32, (n * rows, 128), 1) == me
    gate = jnp.sum(jnp.where(here, all_gates, 0.0), axis=1, keepdims=True)

    def down_body(t, _):
        cols = pl.ds(pl.multiple_of(t * tile, tile), tile)
        o = jnp.dot(act[...], wd[:, cols], preferred_element_type=F32) * gate
        part[:, :, cols] = o.astype(BF16).reshape(n, rows, tile)
        return 0

    lax.fori_loop(0, width // tile, down_body, 0)

    def rs(src, dst, slot, target):
        return pltpu.make_async_remote_copy(
            src_ref=src,
            dst_ref=dst,
            send_sem=rs_s.at[slot],
            recv_sem=rs_r.at[slot],
            device_id={"expert": target},
            device_id_type=MESH,
        )

    def to_sibling(zz, yy):
        slot = zz * 2 + yy
        return rs(part.at[at(zz, yy, 1 - c)], r1.at[slot], slot, sibling)

    def to_y(zz):
        return rs(part.at[at(zz, 1 - y, c)], r2.at[zz], 2 * depth + zz, at(z, 1 - y, c))

    def to_z(d):
        there = at((z + d) % depth, y, c)
        return rs(part.at[there], r3.at[d - 1], 3 * depth + d - 1, there)

    def attend_chip(j):
        src_chip = (chip + chips - j) % chips
        if j == 0:
            own_kv.wait()
            kv(sibling, sibling).wait_recv()
            sc(sibling, sibling).wait_recv()
        else:
            for cc in range(2):
                src = src_chip * 2 + cc
                kv(sibling, src).wait_recv()
                sc(sibling, src).wait_recv()
        span = 2 * tokens
        peer_blocks = tokens // 16
        lanes = lax.broadcasted_iota(jnp.int32, (meta_ref.shape[0], span), 1)
        entry = lax.broadcasted_iota(jnp.int32, (meta_ref.shape[0], span), 0)
        slot = src_chip * 2 * peer_blocks + lanes // 16
        live = jnp.logical_and(
            meta_ref[:, 0:1] == slot, (entry % 4) * 16 + lanes % 16 < meta_ref[:, 1:2]
        )
        owner = jnp.sum(jnp.where(live, entry // 4 + 1, 0), axis=0, keepdims=True) - 1
        pair = pl.ds(src_chip * 2, 2)

        for h in range(heads):
            keys = pool[pair, :, h * HEAD_SIZE : (h + 1) * HEAD_SIZE].reshape(span, HEAD_SIZE)
            vals = pool[pair, :, (heads + h) * HEAD_SIZE : (heads + h + 1) * HEAD_SIZE].reshape(
                span, HEAD_SIZE
            )
            k_scale = jnp.concatenate(
                [scales[src_chip * 2, h : h + 1, :], scales[src_chip * 2 + 1, h : h + 1, :]], axis=1
            ) * (1.0 / math.sqrt(HEAD_SIZE))
            v_scale = jnp.concatenate(
                [
                    scales[src_chip * 2, heads + h : heads + h + 1, :],
                    scales[src_chip * 2 + 1, heads + h : heads + h + 1, :],
                ],
                axis=1,
            )
            step = 128

            def body(t, _):
                rr = pl.ds(pl.multiple_of(t * step, step), step)
                s = lax.dot_general(
                    qh[h, rr, :], keys, (((1,), (1,)), ((), ())), preferred_element_type=F32
                )
                req = lax.broadcasted_iota(jnp.int32, (step, span), 0) % rows
                s = jnp.where(req == owner, s * k_scale, -1e30)
                m_old = m_ref[h, rr, :]
                m_new = jnp.maximum(m_old, jnp.max(s, axis=1, keepdims=True))
                p = jnp.exp(s - jnp.concatenate([m_new, m_new], axis=1))
                alpha = jnp.exp(m_old - m_new)
                m_ref[h, rr, :] = m_new
                l_ref[h, rr, :] = alpha * l_ref[h, rr, :] + p[:, :tokens] + p[:, tokens:]
                mix = jnp.dot((p * v_scale).astype(BF16), vals, preferred_element_type=F32)
                acc[h, rr, :] = alpha * acc[h, rr, :] + mix
                return 0

            lax.fori_loop(0, group * rows // step, body, 0)

    for zz in range(depth):
        to_sibling(zz, 1 - y).start()
    for zz in range(depth):
        to_sibling(zz, y).start()
    attend_chip(0)
    for zz in range(depth):
        to_sibling(zz, 1 - y).wait_recv()
        there = at(zz, 1 - y, c)
        part[there] = (part[there].astype(F32) + r1[zz * 2 + 1 - y].astype(F32)).astype(BF16)
        to_y(zz).start()
    for zz in range(depth):
        to_sibling(zz, y).wait_recv()
        there = at(zz, y, c)
        part[there] = (part[there].astype(F32) + r1[zz * 2 + y].astype(F32)).astype(BF16)
    attend_chip(1)
    for d in range(1, depth):
        zz = (z + d) % depth
        to_y(zz).wait_recv()
        there = at(zz, y, c)
        part[there] = (part[there].astype(F32) + r2[zz].astype(F32)).astype(BF16)
        to_z(d).start()
    to_y(z).wait_recv()
    for j in range(2, chips):
        attend_chip(j)
    total = part[me].astype(F32) + r2[z].astype(F32)
    for d in range(1, depth):
        to_z(d).wait_recv()
        total = total + r3[d - 1].astype(F32)
    moe_ref[...] = total.astype(BF16)

    for h in range(heads):
        for g in range(group):
            rr = slice(g * rows, (g + 1) * rows)
            at_lane = (h * group + g) * HEAD_SIZE
            norm = jnp.sum(l_ref[h, rr, :], axis=1, keepdims=True)
            attn_ref[:, at_lane : at_lane + HEAD_SIZE] = (acc[h, rr, :] / norm).astype(BF16)

    for i in range(n - 1):
        ag(me, i, sibling).wait_send()
    for dest in kv_order:
        sc(dest, me).wait_send()
        kv(dest, me).wait_send()
    for zz in range(depth):
        for yy in range(2):
            to_sibling(zz, yy).wait_send()
        to_y(zz).wait_send()
    for d in range(1, depth):
        to_z(d).wait_send()


def fused_local(
    n,
    queries,
    incoming_key_value,
    key_value_codes,
    key_value_scales,
    lengths,
    block_table,
    hidden,
    routes,
    router,
    w_gate,
    w_up,
    w_down,
):
    rows, width = hidden.shape
    ff = w_gate.shape[2]
    blocks, block_tokens, features = key_value_codes.shape
    tokens = blocks // n * block_tokens
    depth = n // 4
    codes = key_value_codes.reshape(n, tokens, features)
    kinds = key_value_scales.shape[1]
    scales = jnp.transpose(
        key_value_scales.reshape(n, blocks // n, kinds, block_tokens), (0, 2, 1, 3)
    ).reshape(n, kinds, tokens)
    scales = jnp.pad(scales.astype(jnp.float32), ((0, 0), (0, 8 - kinds), (0, 0)))
    table = block_table[0]
    meta = jnp.stack(
        [table.reshape(-1), jnp.broadcast_to(lengths[0][:, None], table.shape).reshape(-1)], axis=1
    )
    q_rows = rows * QUERY_HEADS // KEY_VALUE_HEADS
    vmem = pl.BlockSpec(memory_space=pltpu.VMEM)
    hbm = pl.BlockSpec(memory_space=pl.ANY)
    dma = pltpu.SemaphoreType.DMA
    return pl.pallas_call(
        functools.partial(fused_kernel, n),
        out_shape=(
            jax.ShapeDtypeStruct(queries.shape, BF16),
            jax.ShapeDtypeStruct(hidden.shape, BF16),
        ),
        in_specs=[vmem, vmem, hbm, vmem, vmem, vmem, vmem, vmem, hbm, hbm, hbm],
        out_specs=(vmem, vmem),
        scratch_shapes=[
            pltpu.VMEM((n, rows, width + 128), BF16),
            pltpu.VMEM((n, tokens, features), BF16),
            pltpu.VMEM((n, 8, tokens), F32),
            pltpu.VMEM((width, ff), BF16),
            pltpu.VMEM((width, ff), BF16),
            pltpu.VMEM((ff, width), BF16),
            pltpu.VMEM((n * rows, ff), BF16),
            pltpu.VMEM((n, rows, width), BF16),
            pltpu.VMEM((2 * depth, rows, width), BF16),
            pltpu.VMEM((depth, rows, width), BF16),
            pltpu.VMEM((depth - 1, rows, width), BF16),
            pltpu.VMEM((KEY_VALUE_HEADS, q_rows, HEAD_SIZE), BF16),
            pltpu.VMEM((KEY_VALUE_HEADS, q_rows, HEAD_SIZE), F32),
            pltpu.VMEM((KEY_VALUE_HEADS, q_rows, HEAD_SIZE), F32),
            pltpu.VMEM((KEY_VALUE_HEADS, q_rows, HEAD_SIZE), F32),
            dma((3,)),
            dma((1,)),
            dma((n - 1,)),
            dma((n,)),
            dma((n,)),
            dma((n,)),
            dma((n,)),
            dma((n,)),
            dma((n - 1,)),
            dma((n - 1,)),
        ],
        compiler_params=pltpu.CompilerParams(
            collective_id=0, has_side_effects=True, vmem_limit_bytes=48 * 1024 * 1024
        ),
    )(
        queries,
        incoming_key_value,
        codes,
        scales,
        meta,
        hidden,
        routes,
        router,
        w_gate[0],
        w_up[0],
        w_down[0],
    )


def solution(mesh):
    in_specs = (
        P(("groups", "expert"), None),
        P(("groups", "expert"), None),
        P(("groups", "expert"), None, None),
        P(("groups", "expert"), None, None),
        P(("groups", "expert"), None),
        P(("groups", "expert"), None, None),
        P(("groups", "expert"), None),
        P(("groups", "expert"), None),
        P(),
        P("expert", None, None),
        P("expert", None, None),
        P("expert", None, None),
    )
    out_specs = (P(("groups", "expert"), None), P(("groups", "expert"), None))
    n = mesh.shape["expert"]
    body = functools.partial(fused_local, n) if n == 16 else local
    return jax.shard_map(body, mesh=mesh, in_specs=in_specs, out_specs=out_specs, check_vma=False)
```

```python
import functools
import math

import jax
import jax.numpy as jnp
from jax import lax
from jax.experimental import pallas as pl
from jax.experimental.pallas import tpu as pltpu
from jax.sharding import PartitionSpec as P

QUERY_HEADS = 32
KEY_VALUE_HEADS = 2
HEAD_SIZE = 128


def attend(
    query_row_block,
    newest_key_value,
    device_block_codes,
    device_block_scales,
    prompt_lens,
    block_row_slice,
):
    count_of_rows = query_row_block.shape[0]
    block_list = block_row_slice.shape[1]
    block_length = device_block_codes.shape[1]
    context_tokens = block_list * block_length
    head_groups = QUERY_HEADS // KEY_VALUE_HEADS
    inv_root = 1.0 / math.sqrt(HEAD_SIZE)
    cached_entries = device_block_codes[block_row_slice].reshape(
        count_of_rows, context_tokens, 2, KEY_VALUE_HEADS, HEAD_SIZE
    )
    scale_values = device_block_scales[block_row_slice].reshape(
        count_of_rows, block_list, 2, KEY_VALUE_HEADS, block_length
    )
    scale_values = (
        jnp.transpose(scale_values, (0, 2, 3, 1, 4))
        .reshape(count_of_rows, 2, KEY_VALUE_HEADS, context_tokens)
        .astype(jnp.float32)
    )
    query_head_count = query_row_block.reshape(
        count_of_rows, KEY_VALUE_HEADS, head_groups, HEAD_SIZE
    )
    key_codes = cached_entries[:, :, 0]
    value_codes = cached_entries[:, :, 1]
    raw_dots = jnp.einsum(
        "rhgd,rthd->rhgt", query_head_count, key_codes, preferred_element_type=jnp.float32
    )
    scores = raw_dots * scale_values[:, 0][:, :, None, :] * inv_root
    newest_key = newest_key_value[:, : KEY_VALUE_HEADS * HEAD_SIZE].reshape(
        count_of_rows, KEY_VALUE_HEADS, HEAD_SIZE
    )
    newest_value = (
        newest_key_value[:, KEY_VALUE_HEADS * HEAD_SIZE :]
        .reshape(count_of_rows, KEY_VALUE_HEADS, HEAD_SIZE)
        .astype(jnp.float32)
    )
    own_score = (
        jnp.einsum(
            "rhgd,rhd->rhg", query_head_count, newest_key, preferred_element_type=jnp.float32
        )
        * inv_root
    )
    live_mask = (jnp.arange(context_tokens, dtype=jnp.int32)[None, :] < prompt_lens[:, None])[
        :, None, None, :
    ]
    masked = jnp.where(live_mask, scores, -1e30)
    peak_score = jnp.maximum(jnp.max(masked, axis=-1), own_score)
    exp_terms = jnp.where(live_mask, jnp.exp(masked - peak_score[..., None]), 0.0)
    own_exp = jnp.exp(own_score - peak_score)
    totals = jnp.sum(exp_terms, axis=-1) + own_exp
    weights = (exp_terms / totals[..., None] * scale_values[:, 1][:, :, None, :]).astype(
        jnp.bfloat16
    )
    own_weight = (own_exp / totals).astype(jnp.bfloat16)
    mixture = jnp.einsum(
        "rhgt,rthd->rhgd", weights, value_codes, preferred_element_type=jnp.float32
    )
    mixture = mixture + own_weight.astype(jnp.float32)[..., None] * newest_value[:, :, None, :]
    return mixture.reshape(count_of_rows, QUERY_HEADS * HEAD_SIZE).astype(jnp.bfloat16)


def local(
    queries,
    incoming_key_value,
    key_value_codes,
    key_value_scales,
    lengths,
    block_table,
    hidden,
    routes,
    router,
    w_gate,
    w_up,
    w_down,
):
    count_of_rows = hidden.shape[0]
    top_count = routes.shape[1]
    experts = router.shape[1]
    capacity = 2 * count_of_rows * top_count // experts
    flat_routes = routes.reshape(count_of_rows * top_count)
    columns = jnp.arange(experts, dtype=jnp.int32)
    expert_hits = (flat_routes[:, None] == columns[None, :]).astype(jnp.int32)
    slot_rank = jnp.sum((jnp.cumsum(expert_hits, axis=0) - expert_hits) * expert_hits, axis=1)
    slot_index = flat_routes * capacity + slot_rank
    slot_hot = (
        slot_index[:, None] == jnp.arange(experts * capacity, dtype=jnp.int32)[None, :]
    ).reshape(count_of_rows, top_count, experts * capacity)
    logits = jnp.dot(hidden, router, preferred_element_type=jnp.float32)
    chosen = jnp.sum(
        jnp.where(routes[:, :, None] == columns[None, None, :], logits[:, None, :], 0.0), axis=2
    )
    gate_probs = jax.nn.softmax(chosen, axis=-1).astype(jnp.bfloat16)
    device_block_codes, device_block_scales = (
        lax.all_to_all(key_value_codes, "expert", split_axis=0, concat_axis=0, tiled=True),
        lax.all_to_all(key_value_scales, "expert", split_axis=0, concat_axis=0, tiled=True),
    )
    dispatch_matrix = jnp.any(slot_hot, axis=1).astype(jnp.bfloat16)
    outgoing = jnp.einsum(
        "rs,rd->sd", dispatch_matrix, hidden, preferred_element_type=jnp.float32
    ).astype(jnp.bfloat16)
    received = lax.all_to_all(outgoing, "expert", split_axis=0, concat_axis=0, tiled=True)
    gate_part = jnp.dot(received, w_gate[0], preferred_element_type=jnp.float32)
    up_part = jnp.dot(received, w_up[0], preferred_element_type=jnp.float32)
    inner_act = (jax.nn.silu(gate_part) * up_part).astype(jnp.bfloat16)
    results = jnp.dot(inner_act, w_down[0], preferred_element_type=jnp.float32).astype(jnp.bfloat16)
    returned = lax.all_to_all(results, "expert", split_axis=0, concat_axis=0, tiled=True)
    combine_weights = jnp.sum(
        jnp.where(slot_hot, gate_probs.astype(jnp.float32)[:, :, None], 0.0), axis=1
    ).astype(jnp.bfloat16)
    moe_out = jnp.dot(combine_weights, returned, preferred_element_type=jnp.float32).astype(
        jnp.bfloat16
    )
    attn_out = attend(
        queries,
        incoming_key_value,
        device_block_codes,
        device_block_scales,
        lengths[0],
        block_table[0],
    )
    return (attn_out, moe_out)


MESH = pl.DeviceIdType.MESH
F32 = jnp.float32
LOG2_SCALE = math.log2(math.e) / math.sqrt(HEAD_SIZE)
BF16 = jnp.bfloat16


def fused_kernel(
    n,
    q_hbm,
    new_hbm,
    kv_ref,
    raw_scale_hbm,
    table_hbm,
    lengths_hbm,
    hid_hbm,
    routes_hbm,
    router_hbm,
    wg_hbm,
    wu_hbm,
    wd_hbm,
    attn_ref,
    moe_ref,
    q_ref,
    new_ref,
    raw_scale_ref,
    table_ref,
    lengths_ref,
    routes_ref,
    router_ref,
    scale_ref,
    meta_ref,
    x,
    pool,
    scales,
    wg,
    wu,
    wd,
    act,
    part,
    r1,
    r2,
    r3,
    qh,
    m_ref,
    l_ref,
    acc,
    w_sem,
    own_sem,
    in_sem,
    ag_zs,
    ag_ys,
    ag_cs,
    ag_r,
    kv_s,
    kv_r,
    sc_s,
    sc_r,
    rs_s,
    rs_r,
    rz_s,
    rz_r,
):
    rows, width = hid_hbm.shape
    ff = wg.shape[1]
    experts = router_ref.shape[0]
    depth = n // 4
    chips = n // 2
    heads = KEY_VALUE_HEADS
    group = QUERY_HEADS // heads
    tokens = pool.shape[1]
    me = lax.axis_index("expert")
    z, y, c = me // 4, (me // 2) % 2, me % 2
    chip = me // 2
    sibling = chip * 2 + (1 - c)

    def at(zz, yy, cc):
        return zz * 4 + yy * 2 + cc

    own_x = x.at[me, :, pl.ds(0, width)]
    loads = [
        pltpu.make_async_copy(src, dst, in_sem.at[i])
        for i, (src, dst) in enumerate(
            (
                (hid_hbm, own_x),
                (router_hbm, router_ref),
                (routes_hbm, routes_ref),
                (table_hbm, table_ref),
                (lengths_hbm, lengths_ref),
                (raw_scale_hbm, raw_scale_ref),
                (q_hbm, q_ref),
                (new_hbm, new_ref),
            )
        )
    ]
    for load in loads:
        load.start()
    weights = [
        pltpu.make_async_copy(s, d, w_sem.at[i])
        for i, (s, d) in enumerate(((wg_hbm, wg), (wu_hbm, wu), (wd_hbm, wd)))
    ]
    for w in weights:
        w.start()
    own_kv = pltpu.make_async_copy(kv_ref.at[me], pool.at[me], own_sem.at[0])
    own_kv.start()

    barrier = pltpu.get_barrier_semaphore()
    for k in range(1, n):
        pl.semaphore_signal(
            barrier, inc=1, device_id={"expert": (me + k) % n}, device_id_type=MESH
        )

    for load in loads[:3]:
        load.wait()
    logits = lax.dot_general(
        router_ref[...],
        x[me, :, :width],
        (((1,), (1,)), ((), ())),
        preferred_element_type=F32,
    )
    expert = lax.broadcasted_iota(jnp.int32, (experts, rows), 0)
    chosen = expert < 0
    for k in range(routes_ref.shape[0]):
        chosen = jnp.logical_or(chosen, routes_ref[k : k + 1, :] == expert)
    logits = jnp.where(chosen, logits, -1e30)
    terms = jnp.where(chosen, jnp.exp(logits - jnp.max(logits, axis=0, keepdims=True)), 0.0)
    gates = (terms / jnp.sum(terms, axis=0, keepdims=True)).astype(BF16)
    spread = (
        lax.broadcasted_iota(jnp.int32, (experts, 128), 0)
        == lax.broadcasted_iota(jnp.int32, (experts, 128), 1)
    ).astype(BF16)
    x[me, :, width:] = lax.dot_general(
        gates, spread, (((0,), (0,)), ((), ())), preferred_element_type=F32
    ).astype(BF16)

    pl.semaphore_wait(barrier, n - 1)

    def ag(src, send, target):
        return pltpu.make_async_remote_copy(
            src_ref=x.at[src],
            dst_ref=x.at[src],
            send_sem=send,
            recv_sem=ag_r.at[src],
            device_id={"expert": target},
            device_id_type=MESH,
        )

    def kv(dest, source):
        return pltpu.make_async_remote_copy(
            src_ref=kv_ref.at[dest],
            dst_ref=pool.at[source],
            send_sem=kv_s.at[dest],
            recv_sem=kv_r.at[source],
            device_id={"expert": dest},
            device_id_type=MESH,
        )

    def sc(dest, source):
        return pltpu.make_async_remote_copy(
            src_ref=scale_ref.at[dest],
            dst_ref=scales.at[source],
            send_sem=sc_s.at[dest],
            recv_sem=sc_r.at[source],
            device_id={"expert": dest},
            device_id_type=MESH,
        )

    last = depth - 1

    def ag_up(zz):
        return ag(at(zz, y, c), ag_zs.at[0, zz], at(jnp.minimum(z + 1, last), y, c))

    def ag_down(zz):
        return ag(at(zz, y, c), ag_zs.at[1, zz], at(jnp.maximum(z - 1, 0), y, c))

    def ag_y(zz):
        return ag(at(zz, y, c), ag_ys.at[zz], at(z, 1 - y, c))

    def ag_core(zz, yy):
        return ag(at(zz, yy, c), ag_cs.at[zz * 2 + yy], sibling)

    def arrived(src):
        ag(src, ag_cs.at[0], sibling).wait_recv()

    @pl.when(z < last)
    def _():
        ag_up(z).start()

    @pl.when(z > 0)
    def _():
        ag_down(z).start()

    ag_y(z).start()
    ag_core(z, y).start()

    z_far = ((z + depth // 2) % depth, last - z)
    z_near = (z // 2) * 2 + (1 - z % 2)
    chip_order = [zz * 2 + yy for zz in z_far for yy in (y, 1 - y)]
    chip_order += [z_near * 2 + y, z_near * 2 + 1 - y, z * 2 + 1 - y]
    kv_order = [cc * 2 + k for cc in chip_order for k in (c, 1 - c)] + [sibling]

    for load in loads[3:]:
        load.wait()
    kinds, inner, blocks = raw_scale_ref.shape
    raw = raw_scale_ref[...].reshape(kinds * inner, blocks)
    per_dest = blocks // n
    for dest in range(n):
        pick = (
            lax.broadcasted_iota(jnp.int32, (blocks, tokens), 0)
            == dest * per_dest + lax.broadcasted_iota(jnp.int32, (blocks, tokens), 1) // inner
        ).astype(BF16)
        wide = jnp.dot(raw, pick, preferred_element_type=F32).reshape(kinds, inner, tokens)
        keep = lax.broadcasted_iota(jnp.int32, (kinds, inner, tokens), 1) == (
            lax.broadcasted_iota(jnp.int32, (kinds, inner, tokens), 2) % inner
        )
        scale_ref[dest, 0:kinds, :] = jnp.sum(jnp.where(keep, wide, 0.0), axis=1)
        scale_ref[dest, kinds:, :] = jnp.zeros((8 - kinds, tokens), F32)
    for dest in kv_order:
        sc(dest, me).start()
    scales[me] = scale_ref[me]
    eye = lax.broadcasted_iota(jnp.int32, (rows, rows), 0) == lax.broadcasted_iota(
        jnp.int32, (rows, rows), 1
    )
    length_col = jnp.sum(jnp.where(eye, lengths_ref[...], 0), axis=1, keepdims=True)
    for b in range(table_ref.shape[0]):
        rr = slice(b * rows, (b + 1) * rows)
        col = jnp.sum(jnp.where(eye, table_ref[b : b + 1, :], 0), axis=1, keepdims=True)
        meta_ref[0, rr, :] = jnp.broadcast_to(col, (rows, 128))
        meta_ref[1, rr, :] = jnp.broadcast_to(length_col - b * 16, (rows, 128))

    req_of_row = lax.broadcasted_iota(jnp.int32, (group * rows, 1), 0) % rows
    for h in range(heads):
        for g in range(group):
            at_lane = (h * group + g) * HEAD_SIZE
            qh[h, g * rows : (g + 1) * rows, :] = q_ref[:, at_lane : at_lane + HEAD_SIZE]
        k_new = new_ref[:, h * HEAD_SIZE : (h + 1) * HEAD_SIZE].astype(F32)
        v_new = new_ref[:, (heads + h) * HEAD_SIZE : (heads + h + 1) * HEAD_SIZE].astype(F32)
        for g in range(group):
            own = jnp.sum(
                qh[h, g * rows : (g + 1) * rows, :].astype(F32) * k_new, axis=1, keepdims=True
            ) * LOG2_SCALE
            m_ref[h, g * rows : (g + 1) * rows, :] = jnp.broadcast_to(own, (rows, HEAD_SIZE))
            acc[h, g * rows : (g + 1) * rows, :] = v_new
        first = lax.broadcasted_iota(jnp.int32, (group * rows, HEAD_SIZE), 1) == 0
        l_ref[h] = jnp.where(first, 1.0, 0.0)

    for d in range(1, depth):

        @pl.when(z >= d)
        def _():
            zz = jnp.maximum(z - d, 0)
            arrived(at(zz, y, c))

            @pl.when(z < last)
            def _():
                ag_up(zz).start()

            ag_y(zz).start()
            ag_core(zz, y).start()

        @pl.when(z + d <= last)
        def _():
            zz = jnp.minimum(z + d, last)
            arrived(at(zz, y, c))

            @pl.when(z > 0)
            def _():
                ag_down(zz).start()

            ag_y(zz).start()
            ag_core(zz, y).start()

    def from_y(zz):
        arrived(at(zz, 1 - y, c))
        ag_core(zz, 1 - y).start()

    from_y(z)
    for d in range(1, depth):

        @pl.when(z >= d)
        def _():
            from_y(jnp.maximum(z - d, 0))

        @pl.when(z + d <= last)
        def _():
            from_y(jnp.minimum(z + d, last))

    for dest in kv_order[0:15]:
        kv(dest, me).start()
    for zz in range(depth):
        for yy in range(2):
            arrived(at(zz, yy, 1 - c))

    weights[0].wait()
    weights[1].wait()
    tile = 256

    def up_body(t, _):
        cols = pl.ds(pl.multiple_of(t * tile, tile), tile)
        xs = x[:, :, :width].reshape(n * rows, width)
        g = jnp.dot(xs, wg[:, cols], preferred_element_type=F32)
        u = jnp.dot(xs, wu[:, cols], preferred_element_type=F32)
        act[:, cols] = (g / (1.0 + jnp.exp(-g)) * u).astype(BF16)
        return 0

    lax.fori_loop(0, ff // tile, up_body, 0)
    weights[2].wait()
    all_gates = x[:, :, width:].reshape(n * rows, 128).astype(F32)
    here = lax.broadcasted_iota(jnp.int32, (n * rows, 128), 1) == me
    gate = jnp.sum(jnp.where(here, all_gates, 0.0), axis=1, keepdims=True)

    def down_body(t, _):
        cols = pl.ds(pl.multiple_of(t * tile, tile), tile)
        o = jnp.dot(act[...], wd[:, cols], preferred_element_type=F32) * gate
        part[:, :, cols] = o.astype(BF16).reshape(n, rows, tile)
        return 0

    lax.fori_loop(0, width // tile, down_body, 0)

    def rs(src, dst, slot, target):
        return pltpu.make_async_remote_copy(
            src_ref=src,
            dst_ref=dst,
            send_sem=rs_s.at[slot],
            recv_sem=rs_r.at[slot],
            device_id={"expert": target},
            device_id_type=MESH,
        )

    def to_sibling(zz, yy):
        slot = zz * 2 + yy
        return rs(part.at[at(zz, yy, 1 - c)], r1.at[slot], slot, sibling)

    def to_y(zz):
        return rs(part.at[at(zz, 1 - y, c)], r2.at[zz], 2 * depth + zz, at(z, 1 - y, c))

    def rz(way, zt):
        target = jnp.minimum(z + 1, last) if way == 0 else jnp.maximum(z - 1, 0)
        return pltpu.make_async_remote_copy(
            src_ref=part.at[at(zt, y, c)],
            dst_ref=r3.at[way, zt],
            send_sem=rz_s.at[way, zt],
            recv_sem=rz_r.at[way, zt],
            device_id={"expert": at(target, y, c)},
            device_id_type=MESH,
        )

    def step_z(way, zt):
        ahead = z < zt if way == 0 else z > zt
        inner_device = z > 0 if way == 0 else z < last

        @pl.when(ahead)
        def _():
            @pl.when(inner_device)
            def _():
                rz(way, zt).wait_recv()
                there = at(zt, y, c)
                part[there] = (part[there].astype(F32) + r3[way, zt].astype(F32)).astype(BF16)

            rz(way, zt).start()

    def attend_chip(j):
        src_chip = chip if j == 0 else chip_order[j - 1]
        if j == 0:
            own_kv.wait()
            kv(sibling, sibling).wait_recv()
            sc(sibling, sibling).wait_recv()
        else:
            for cc in range(2):
                src = src_chip * 2 + cc
                kv(sibling, src).wait_recv()
                sc(sibling, src).wait_recv()
        span = 2 * tokens
        peer_blocks = tokens // 16
        lanes = lax.broadcasted_iota(jnp.int32, (meta_ref.shape[1], span), 1)
        entry = lax.broadcasted_iota(jnp.int32, (meta_ref.shape[1], span), 0)
        slot = src_chip * 2 * peer_blocks + lanes // 16
        live = jnp.logical_and(
            meta_ref[0, :, 0:1] == slot, lanes % 16 < meta_ref[1, :, 0:1]
        )
        owner = jnp.sum(jnp.where(live, entry % rows + 1, 0), axis=0, keepdims=True) - 1
        pair = pl.ds(src_chip * 2, 2)

        for h in range(heads):
            keys = pool[pair, :, h * HEAD_SIZE : (h + 1) * HEAD_SIZE].reshape(span, HEAD_SIZE)
            vals = pool[pair, :, (heads + h) * HEAD_SIZE : (heads + h + 1) * HEAD_SIZE].reshape(
                span, HEAD_SIZE
            )
            k_scale = jnp.concatenate(
                [scales[src_chip * 2, h : h + 1, :], scales[src_chip * 2 + 1, h : h + 1, :]], axis=1
            ) * LOG2_SCALE
            v_scale = jnp.concatenate(
                [
                    scales[src_chip * 2, heads + h : heads + h + 1, :],
                    scales[src_chip * 2 + 1, heads + h : heads + h + 1, :],
                ],
                axis=1,
            )
            step = 128

            def body(t, _):
                rr = pl.ds(t * step, step)
                s = lax.dot_general(
                    qh[h, rr, :], keys, (((1,), (1,)), ((), ())), preferred_element_type=F32
                )
                req = lax.broadcasted_iota(jnp.int32, (step, span), 0) % rows
                s = jnp.where(req == owner, s * k_scale, -1e30)
                m_old = m_ref[h, rr, :]
                m_new = jnp.maximum(m_old, jnp.max(s, axis=1, keepdims=True))
                p = jnp.exp2(s - jnp.concatenate([m_new, m_new], axis=1))
                alpha = jnp.exp2(m_old - m_new)
                m_ref[h, rr, :] = m_new
                l_ref[h, rr, :] = alpha * l_ref[h, rr, :] + p[:, :tokens] + p[:, tokens:]
                mix = jnp.dot((p * v_scale).astype(BF16), vals, preferred_element_type=F32)
                acc[h, rr, :] = alpha * acc[h, rr, :] + mix
                return 0

            lax.fori_loop(0, group * rows // step, body, 0, unroll=True)

    for zz in range(depth):
        to_sibling(zz, 1 - y).start()
    for zz in range(depth):
        to_sibling(zz, y).start()
    attend_chip(0)
    for zz in range(depth):
        to_sibling(zz, 1 - y).wait_recv()
        there = at(zz, 1 - y, c)
        part[there] = (part[there].astype(F32) + r1[zz * 2 + 1 - y].astype(F32)).astype(BF16)
        to_y(zz).start()
    for zz in range(depth):
        to_sibling(zz, y).wait_recv()
        there = at(zz, y, c)
        part[there] = (part[there].astype(F32) + r1[zz * 2 + y].astype(F32)).astype(BF16)
    attend_chip(1)
    for zz in range(depth):
        to_y(zz).wait_recv()
        there = at(zz, y, c)
        part[there] = (part[there].astype(F32) + r2[zz].astype(F32)).astype(BF16)

        @pl.when(jnp.logical_and(z == 0, zz > 0))
        def _():
            if zz > 0:
                step_z(0, zz)

        @pl.when(jnp.logical_and(z == last, zz < last))
        def _():
            if zz < last:
                step_z(1, zz)

    @pl.when(z > 0)
    def _():
        for zt in range(last, 0, -1):
            step_z(0, zt)

    @pl.when(z < last)
    def _():
        for zt in range(last):
            step_z(1, zt)

    for j in range(2, chips):
        attend_chip(j)
    @pl.when(z > 0)
    def _():
        rz(0, z).wait_recv()
        r1[0] = r3[0, z]

    @pl.when(z == 0)
    def _():
        r1[0] = jnp.zeros((rows, width), BF16)

    @pl.when(z < last)
    def _():
        rz(1, z).wait_recv()
        r1[1] = r3[1, z]

    @pl.when(z == last)
    def _():
        r1[1] = jnp.zeros((rows, width), BF16)

    moe_ref[...] = (part[me].astype(F32) + r1[0].astype(F32) + r1[1].astype(F32)).astype(BF16)

    for h in range(heads):
        for g in range(group):
            rr = slice(g * rows, (g + 1) * rows)
            at_lane = (h * group + g) * HEAD_SIZE
            norm = jnp.sum(l_ref[h, rr, :], axis=1, keepdims=True)
            attn_ref[:, at_lane : at_lane + HEAD_SIZE] = (acc[h, rr, :] / norm).astype(BF16)

    for zz in range(depth):

        @pl.when(jnp.logical_and(z < last, zz <= z))
        def _():
            ag_up(zz).wait_send()

        @pl.when(jnp.logical_and(z > 0, zz >= z))
        def _():
            ag_down(zz).wait_send()

        ag_y(zz).wait_send()
        for yy in range(2):
            ag_core(zz, yy).wait_send()
    for dest in kv_order:
        sc(dest, me).wait_send()
        kv(dest, me).wait_send()
    for zz in range(depth):
        for yy in range(2):
            to_sibling(zz, yy).wait_send()
        to_y(zz).wait_send()
    for zt in range(depth):

        @pl.when(z < zt)
        def _():
            rz(0, zt).wait_send()

        @pl.when(z > zt)
        def _():
            rz(1, zt).wait_send()


def fused_local(
    n,
    queries,
    incoming_key_value,
    key_value_codes,
    key_value_scales,
    lengths,
    block_table,
    hidden,
    routes,
    router,
    w_gate,
    w_up,
    w_down,
):
    rows, width = hidden.shape
    ff = w_gate.shape[2]
    blocks, block_tokens, features = key_value_codes.shape
    tokens = blocks // n * block_tokens
    depth = n // 4
    codes = key_value_codes.reshape(n, tokens, features)
    kinds = key_value_scales.shape[1]
    per_request = block_table.shape[2]
    q_rows = rows * QUERY_HEADS // KEY_VALUE_HEADS
    vmem = pl.BlockSpec(memory_space=pltpu.VMEM)
    hbm = pl.BlockSpec(memory_space=pltpu.HBM)
    dma = pltpu.SemaphoreType.DMA
    return pl.pallas_call(
        functools.partial(fused_kernel, n),
        out_shape=(
            jax.ShapeDtypeStruct(queries.shape, BF16),
            jax.ShapeDtypeStruct(hidden.shape, BF16),
        ),
        in_specs=[hbm] * 12,
        out_specs=(vmem, vmem),
        scratch_shapes=[
            pltpu.VMEM(queries.shape, BF16),
            pltpu.VMEM(incoming_key_value.shape, BF16),
            pltpu.VMEM((kinds, block_tokens, blocks), BF16),
            pltpu.VMEM((per_request, rows), jnp.int32),
            pltpu.VMEM((1, rows), jnp.int32),
            pltpu.VMEM((routes.shape[1], rows), jnp.int32),
            pltpu.VMEM((router.shape[1], width), BF16),
            pltpu.VMEM((n, 8, tokens), F32),
            pltpu.VMEM((2, per_request * rows, 128), jnp.int32),
            pltpu.VMEM((n, rows, width + 128), BF16),
            pltpu.VMEM((n, tokens, features), BF16),
            pltpu.VMEM((n, 8, tokens), F32),
            pltpu.VMEM((width, ff), BF16),
            pltpu.VMEM((width, ff), BF16),
            pltpu.VMEM((ff, width), BF16),
            pltpu.VMEM((n * rows, ff), BF16),
            pltpu.VMEM((n, rows, width), BF16),
            pltpu.VMEM((2 * depth, rows, width), BF16),
            pltpu.VMEM((depth, rows, width), BF16),
            pltpu.VMEM((2, depth, rows, width), BF16),
            pltpu.VMEM((KEY_VALUE_HEADS, q_rows, HEAD_SIZE), BF16),
            pltpu.VMEM((KEY_VALUE_HEADS, q_rows, HEAD_SIZE), F32),
            pltpu.VMEM((KEY_VALUE_HEADS, q_rows, HEAD_SIZE), F32),
            pltpu.VMEM((KEY_VALUE_HEADS, q_rows, HEAD_SIZE), F32),
            dma((3,)),
            dma((1,)),
            dma((8,)),
            dma((2, depth)),
            dma((depth,)),
            dma((2 * depth,)),
            dma((n,)),
            dma((n,)),
            dma((n,)),
            dma((n,)),
            dma((n,)),
            dma((3 * depth,)),
            dma((3 * depth,)),
            dma((2, depth)),
            dma((2, depth)),
        ],
        compiler_params=pltpu.CompilerParams(
            collective_id=0, has_side_effects=True, vmem_limit_bytes=63 * 1024 * 1024
        ),
    )(
        queries,
        incoming_key_value,
        codes,
        jnp.transpose(key_value_scales, (1, 2, 0)),
        jnp.transpose(block_table[0]),
        lengths,
        hidden,
        jnp.transpose(routes),
        jnp.transpose(router),
        w_gate[0],
        w_up[0],
        w_down[0],
    )


def solution(mesh):
    in_specs = (
        P(("groups", "expert"), None),
        P(("groups", "expert"), None),
        P(("groups", "expert"), None, None),
        P(("groups", "expert"), None, None),
        P(("groups", "expert"), None),
        P(("groups", "expert"), None, None),
        P(("groups", "expert"), None),
        P(("groups", "expert"), None),
        P(),
        P("expert", None, None),
        P("expert", None, None),
        P("expert", None, None),
    )
    out_specs = (P(("groups", "expert"), None), P(("groups", "expert"), None))
    n = mesh.shape["expert"]
    body = functools.partial(fused_local, n) if n == 16 else local
    return jax.shard_map(body, mesh=mesh, in_specs=in_specs, out_specs=out_specs, check_vma=False)
```

```python
import functools
import math

import jax
import jax.numpy as jnp
from jax import lax
from jax.experimental import pallas as pl
from jax.experimental.pallas import tpu as pltpu
from jax.sharding import PartitionSpec as P

QUERY_HEADS = 32
KEY_VALUE_HEADS = 2
HEAD_SIZE = 128


def attend(
    query_row_block,
    newest_key_value,
    device_block_codes,
    device_block_scales,
    prompt_lens,
    block_row_slice,
):
    count_of_rows = query_row_block.shape[0]
    block_list = block_row_slice.shape[1]
    block_length = device_block_codes.shape[1]
    context_tokens = block_list * block_length
    head_groups = QUERY_HEADS // KEY_VALUE_HEADS
    inv_root = 1.0 / math.sqrt(HEAD_SIZE)
    cached_entries = device_block_codes[block_row_slice].reshape(
        count_of_rows, context_tokens, 2, KEY_VALUE_HEADS, HEAD_SIZE
    )
    scale_values = device_block_scales[block_row_slice].reshape(
        count_of_rows, block_list, 2, KEY_VALUE_HEADS, block_length
    )
    scale_values = (
        jnp.transpose(scale_values, (0, 2, 3, 1, 4))
        .reshape(count_of_rows, 2, KEY_VALUE_HEADS, context_tokens)
        .astype(jnp.float32)
    )
    query_head_count = query_row_block.reshape(
        count_of_rows, KEY_VALUE_HEADS, head_groups, HEAD_SIZE
    )
    key_codes = cached_entries[:, :, 0]
    value_codes = cached_entries[:, :, 1]
    raw_dots = jnp.einsum(
        "rhgd,rthd->rhgt", query_head_count, key_codes, preferred_element_type=jnp.float32
    )
    scores = raw_dots * scale_values[:, 0][:, :, None, :] * inv_root
    newest_key = newest_key_value[:, : KEY_VALUE_HEADS * HEAD_SIZE].reshape(
        count_of_rows, KEY_VALUE_HEADS, HEAD_SIZE
    )
    newest_value = (
        newest_key_value[:, KEY_VALUE_HEADS * HEAD_SIZE :]
        .reshape(count_of_rows, KEY_VALUE_HEADS, HEAD_SIZE)
        .astype(jnp.float32)
    )
    own_score = (
        jnp.einsum(
            "rhgd,rhd->rhg", query_head_count, newest_key, preferred_element_type=jnp.float32
        )
        * inv_root
    )
    live_mask = (jnp.arange(context_tokens, dtype=jnp.int32)[None, :] < prompt_lens[:, None])[
        :, None, None, :
    ]
    masked = jnp.where(live_mask, scores, -1e30)
    peak_score = jnp.maximum(jnp.max(masked, axis=-1), own_score)
    exp_terms = jnp.where(live_mask, jnp.exp(masked - peak_score[..., None]), 0.0)
    own_exp = jnp.exp(own_score - peak_score)
    totals = jnp.sum(exp_terms, axis=-1) + own_exp
    weights = (exp_terms / totals[..., None] * scale_values[:, 1][:, :, None, :]).astype(
        jnp.bfloat16
    )
    own_weight = (own_exp / totals).astype(jnp.bfloat16)
    mixture = jnp.einsum(
        "rhgt,rthd->rhgd", weights, value_codes, preferred_element_type=jnp.float32
    )
    mixture = mixture + own_weight.astype(jnp.float32)[..., None] * newest_value[:, :, None, :]
    return mixture.reshape(count_of_rows, QUERY_HEADS * HEAD_SIZE).astype(jnp.bfloat16)


def local(
    queries,
    incoming_key_value,
    key_value_codes,
    key_value_scales,
    lengths,
    block_table,
    hidden,
    routes,
    router,
    w_gate,
    w_up,
    w_down,
):
    count_of_rows = hidden.shape[0]
    top_count = routes.shape[1]
    experts = router.shape[1]
    capacity = 2 * count_of_rows * top_count // experts
    flat_routes = routes.reshape(count_of_rows * top_count)
    columns = jnp.arange(experts, dtype=jnp.int32)
    expert_hits = (flat_routes[:, None] == columns[None, :]).astype(jnp.int32)
    slot_rank = jnp.sum((jnp.cumsum(expert_hits, axis=0) - expert_hits) * expert_hits, axis=1)
    slot_index = flat_routes * capacity + slot_rank
    slot_hot = (
        slot_index[:, None] == jnp.arange(experts * capacity, dtype=jnp.int32)[None, :]
    ).reshape(count_of_rows, top_count, experts * capacity)
    logits = jnp.dot(hidden, router, preferred_element_type=jnp.float32)
    chosen = jnp.sum(
        jnp.where(routes[:, :, None] == columns[None, None, :], logits[:, None, :], 0.0), axis=2
    )
    gate_probs = jax.nn.softmax(chosen, axis=-1).astype(jnp.bfloat16)
    device_block_codes, device_block_scales = (
        lax.all_to_all(key_value_codes, "expert", split_axis=0, concat_axis=0, tiled=True),
        lax.all_to_all(key_value_scales, "expert", split_axis=0, concat_axis=0, tiled=True),
    )
    dispatch_matrix = jnp.any(slot_hot, axis=1).astype(jnp.bfloat16)
    outgoing = jnp.einsum(
        "rs,rd->sd", dispatch_matrix, hidden, preferred_element_type=jnp.float32
    ).astype(jnp.bfloat16)
    received = lax.all_to_all(outgoing, "expert", split_axis=0, concat_axis=0, tiled=True)
    gate_part = jnp.dot(received, w_gate[0], preferred_element_type=jnp.float32)
    up_part = jnp.dot(received, w_up[0], preferred_element_type=jnp.float32)
    inner_act = (jax.nn.silu(gate_part) * up_part).astype(jnp.bfloat16)
    results = jnp.dot(inner_act, w_down[0], preferred_element_type=jnp.float32).astype(jnp.bfloat16)
    returned = lax.all_to_all(results, "expert", split_axis=0, concat_axis=0, tiled=True)
    combine_weights = jnp.sum(
        jnp.where(slot_hot, gate_probs.astype(jnp.float32)[:, :, None], 0.0), axis=1
    ).astype(jnp.bfloat16)
    moe_out = jnp.dot(combine_weights, returned, preferred_element_type=jnp.float32).astype(
        jnp.bfloat16
    )
    attn_out = attend(
        queries,
        incoming_key_value,
        device_block_codes,
        device_block_scales,
        lengths[0],
        block_table[0],
    )
    return (attn_out, moe_out)


MESH = pl.DeviceIdType.MESH
F32 = jnp.float32
LOG2_SCALE = math.log2(math.e) / math.sqrt(HEAD_SIZE)
BF16 = jnp.bfloat16


def fused_kernel(
    n,
    q_hbm,
    new_hbm,
    kv_ref,
    raw_scale_hbm,
    table_hbm,
    lengths_hbm,
    hid_hbm,
    routes_hbm,
    router_hbm,
    wg_hbm,
    wu_hbm,
    wd_hbm,
    attn_ref,
    moe_ref,
    q_ref,
    new_ref,
    raw_scale_ref,
    table_ref,
    lengths_ref,
    routes_ref,
    router_ref,
    scale_ref,
    meta_ref,
    x,
    pool,
    scales,
    wg,
    wu,
    wd,
    act,
    part,
    r1,
    r2,
    r3,
    qh,
    m_ref,
    l_ref,
    acc,
    w_sem,
    own_sem,
    in_sem,
    ag_zs,
    ag_ys,
    ag_cs,
    ag_r,
    kv_s,
    kv_r,
    sc_s,
    sc_r,
    rs_s,
    rs_r,
):
    rows, width = hid_hbm.shape
    ff = wg.shape[1]
    experts = router_ref.shape[0]
    depth = n // 4
    chips = n // 2
    heads = KEY_VALUE_HEADS
    group = QUERY_HEADS // heads
    tokens = pool.shape[1]
    me = lax.axis_index("expert")
    z, y, c = me // 4, (me // 2) % 2, me % 2
    chip = me // 2
    sibling = chip * 2 + (1 - c)

    def at(zz, yy, cc):
        return zz * 4 + yy * 2 + cc

    own_x = x.at[me, :, pl.ds(0, width)]
    loads = [
        pltpu.make_async_copy(src, dst, in_sem.at[i])
        for i, (src, dst) in enumerate(
            (
                (hid_hbm, own_x),
                (router_hbm, router_ref),
                (routes_hbm, routes_ref),
                (table_hbm, table_ref),
                (lengths_hbm, lengths_ref),
                (raw_scale_hbm, raw_scale_ref),
                (q_hbm, q_ref),
                (new_hbm, new_ref),
            )
        )
    ]
    for load in loads:
        load.start()
    weights = [
        pltpu.make_async_copy(s, d, w_sem.at[i])
        for i, (s, d) in enumerate(((wg_hbm, wg), (wu_hbm, wu), (wd_hbm, wd)))
    ]
    for w in weights:
        w.start()
    own_kv = pltpu.make_async_copy(kv_ref.at[me], pool.at[me], own_sem.at[0])
    own_kv.start()

    barrier = pltpu.get_barrier_semaphore()
    for k in range(1, n):
        pl.semaphore_signal(
            barrier, inc=1, device_id={"expert": (me + k) % n}, device_id_type=MESH
        )

    for load in loads[:3]:
        load.wait()
    logits = lax.dot_general(
        router_ref[...],
        x[me, :, :width],
        (((1,), (1,)), ((), ())),
        preferred_element_type=F32,
    )
    expert = lax.broadcasted_iota(jnp.int32, (experts, rows), 0)
    chosen = expert < 0
    for k in range(routes_ref.shape[0]):
        chosen = jnp.logical_or(chosen, routes_ref[k : k + 1, :] == expert)
    logits = jnp.where(chosen, logits, -1e30)
    terms = jnp.where(chosen, jnp.exp(logits - jnp.max(logits, axis=0, keepdims=True)), 0.0)
    gates = (terms / jnp.sum(terms, axis=0, keepdims=True)).astype(BF16)
    spread = (
        lax.broadcasted_iota(jnp.int32, (experts, 128), 0)
        == lax.broadcasted_iota(jnp.int32, (experts, 128), 1)
    ).astype(BF16)
    x[me, :, width:] = lax.dot_general(
        gates, spread, (((0,), (0,)), ((), ())), preferred_element_type=F32
    ).astype(BF16)

    pl.semaphore_wait(barrier, n - 1)

    def ag(src, send, target):
        return pltpu.make_async_remote_copy(
            src_ref=x.at[src],
            dst_ref=x.at[src],
            send_sem=send,
            recv_sem=ag_r.at[src],
            device_id={"expert": target},
            device_id_type=MESH,
        )

    def kv(dest, source):
        return pltpu.make_async_remote_copy(
            src_ref=kv_ref.at[dest],
            dst_ref=pool.at[source],
            send_sem=kv_s.at[dest],
            recv_sem=kv_r.at[source],
            device_id={"expert": dest},
            device_id_type=MESH,
        )

    def sc(dest, source):
        return pltpu.make_async_remote_copy(
            src_ref=scale_ref.at[dest],
            dst_ref=scales.at[source],
            send_sem=sc_s.at[dest],
            recv_sem=sc_r.at[source],
            device_id={"expert": dest},
            device_id_type=MESH,
        )

    last = depth - 1

    def ag_up(zz):
        return ag(at(zz, y, c), ag_zs.at[0, zz], at(jnp.minimum(z + 1, last), y, c))

    def ag_down(zz):
        return ag(at(zz, y, c), ag_zs.at[1, zz], at(jnp.maximum(z - 1, 0), y, c))

    def ag_y(zz):
        return ag(at(zz, y, c), ag_ys.at[zz], at(z, 1 - y, c))

    def ag_core(zz, yy):
        return ag(at(zz, yy, c), ag_cs.at[zz * 2 + yy], sibling)

    def arrived(src):
        ag(src, ag_cs.at[0], sibling).wait_recv()

    @pl.when(z < last)
    def _():
        ag_up(z).start()

    @pl.when(z > 0)
    def _():
        ag_down(z).start()

    ag_y(z).start()
    ag_core(z, y).start()

    z_far = ((z + depth // 2) % depth, last - z)
    z_near = (z // 2) * 2 + (1 - z % 2)
    chip_order = [zz * 2 + yy for zz in z_far for yy in (y, 1 - y)]
    chip_order += [z_near * 2 + y, z_near * 2 + 1 - y, z * 2 + 1 - y]
    kv_order = [cc * 2 + k for cc in chip_order for k in (c, 1 - c)] + [sibling]

    for load in loads[3:]:
        load.wait()
    kinds, inner, blocks = raw_scale_ref.shape
    raw = raw_scale_ref[...].reshape(kinds * inner, blocks)
    per_dest = blocks // n
    for dest in range(n):
        pick = (
            lax.broadcasted_iota(jnp.int32, (blocks, tokens), 0)
            == dest * per_dest + lax.broadcasted_iota(jnp.int32, (blocks, tokens), 1) // inner
        ).astype(BF16)
        wide = jnp.dot(raw, pick, preferred_element_type=F32).reshape(kinds, inner, tokens)
        keep = lax.broadcasted_iota(jnp.int32, (kinds, inner, tokens), 1) == (
            lax.broadcasted_iota(jnp.int32, (kinds, inner, tokens), 2) % inner
        )
        scale_ref[dest, 0:kinds, :] = jnp.sum(jnp.where(keep, wide, 0.0), axis=1)
        scale_ref[dest, kinds:, :] = jnp.zeros((8 - kinds, tokens), F32)
    for dest in kv_order:
        sc(dest, me).start()
    scales[me] = scale_ref[me]
    eye = lax.broadcasted_iota(jnp.int32, (rows, rows), 0) == lax.broadcasted_iota(
        jnp.int32, (rows, rows), 1
    )
    length_col = jnp.sum(jnp.where(eye, lengths_ref[...], 0), axis=1, keepdims=True)
    for b in range(table_ref.shape[0]):
        rr = slice(b * rows, (b + 1) * rows)
        col = jnp.sum(jnp.where(eye, table_ref[b : b + 1, :], 0), axis=1, keepdims=True)
        meta_ref[0, rr, :] = jnp.broadcast_to(col, (rows, 128))
        meta_ref[1, rr, :] = jnp.broadcast_to(length_col - b * 16, (rows, 128))

    req_of_row = lax.broadcasted_iota(jnp.int32, (group * rows, 1), 0) % rows
    for h in range(heads):
        for g in range(group):
            at_lane = (h * group + g) * HEAD_SIZE
            qh[h, g * rows : (g + 1) * rows, :] = q_ref[:, at_lane : at_lane + HEAD_SIZE]
        k_new = new_ref[:, h * HEAD_SIZE : (h + 1) * HEAD_SIZE].astype(F32)
        v_new = new_ref[:, (heads + h) * HEAD_SIZE : (heads + h + 1) * HEAD_SIZE].astype(F32)
        for g in range(group):
            own = jnp.sum(
                qh[h, g * rows : (g + 1) * rows, :].astype(F32) * k_new, axis=1, keepdims=True
            ) * LOG2_SCALE
            m_ref[h, g * rows : (g + 1) * rows, :] = jnp.broadcast_to(own, (rows, HEAD_SIZE))
            acc[h, g * rows : (g + 1) * rows, :] = v_new
        first = lax.broadcasted_iota(jnp.int32, (group * rows, HEAD_SIZE), 1) == 0
        l_ref[h] = jnp.where(first, 1.0, 0.0)

    for d in range(1, depth):

        @pl.when(z >= d)
        def _():
            zz = jnp.maximum(z - d, 0)
            arrived(at(zz, y, c))

            @pl.when(z < last)
            def _():
                ag_up(zz).start()

            ag_y(zz).start()
            ag_core(zz, y).start()

        @pl.when(z + d <= last)
        def _():
            zz = jnp.minimum(z + d, last)
            arrived(at(zz, y, c))

            @pl.when(z > 0)
            def _():
                ag_down(zz).start()

            ag_y(zz).start()
            ag_core(zz, y).start()

    def from_y(zz):
        arrived(at(zz, 1 - y, c))
        ag_core(zz, 1 - y).start()

    from_y(z)
    for d in range(1, depth):

        @pl.when(z >= d)
        def _():
            from_y(jnp.maximum(z - d, 0))

        @pl.when(z + d <= last)
        def _():
            from_y(jnp.minimum(z + d, last))

    for dest in kv_order[0:15]:
        kv(dest, me).start()
    for zz in range(depth):
        for yy in range(2):
            arrived(at(zz, yy, 1 - c))

    weights[0].wait()
    weights[1].wait()
    tile = 256

    def up_body(t, _):
        cols = pl.ds(pl.multiple_of(t * tile, tile), tile)
        xs = x[:, :, :width].reshape(n * rows, width)
        g = jnp.dot(xs, wg[:, cols], preferred_element_type=F32)
        u = jnp.dot(xs, wu[:, cols], preferred_element_type=F32)
        act[:, cols] = (g / (1.0 + jnp.exp(-g)) * u).astype(BF16)
        return 0

    lax.fori_loop(0, ff // tile, up_body, 0)
    weights[2].wait()
    all_gates = x[:, :, width:].reshape(n * rows, 128).astype(F32)
    here = lax.broadcasted_iota(jnp.int32, (n * rows, 128), 1) == me
    gate = jnp.sum(jnp.where(here, all_gates, 0.0), axis=1, keepdims=True)

    def down_body(t, _):
        cols = pl.ds(pl.multiple_of(t * tile, tile), tile)
        o = jnp.dot(act[...], wd[:, cols], preferred_element_type=F32) * gate
        part[:, :, cols] = o.astype(BF16).reshape(n, rows, tile)
        return 0

    lax.fori_loop(0, width // tile, down_body, 0)

    def rs(src, dst, slot, target):
        return pltpu.make_async_remote_copy(
            src_ref=src,
            dst_ref=dst,
            send_sem=rs_s.at[slot],
            recv_sem=rs_r.at[slot],
            device_id={"expert": target},
            device_id_type=MESH,
        )

    def to_sibling(zz, yy):
        slot = zz * 2 + yy
        return rs(part.at[at(zz, yy, 1 - c)], r1.at[slot], slot, sibling)

    def to_y(zz):
        return rs(part.at[at(zz, 1 - y, c)], r2.at[zz], 2 * depth + zz, at(z, 1 - y, c))

    def to_z(d):
        there = at((z + d) % depth, y, c)
        return rs(part.at[there], r3.at[d - 1], 3 * depth + d - 1, there)

    def attend_chip(j):
        src_chip = chip if j == 0 else chip_order[j - 1]
        if j == 0:
            own_kv.wait()
            kv(sibling, sibling).wait_recv()
            sc(sibling, sibling).wait_recv()
        else:
            for cc in range(2):
                src = src_chip * 2 + cc
                kv(sibling, src).wait_recv()
                sc(sibling, src).wait_recv()
        span = 2 * tokens
        peer_blocks = tokens // 16
        lanes = lax.broadcasted_iota(jnp.int32, (meta_ref.shape[1], span), 1)
        entry = lax.broadcasted_iota(jnp.int32, (meta_ref.shape[1], span), 0)
        slot = src_chip * 2 * peer_blocks + lanes // 16
        live = jnp.logical_and(
            meta_ref[0, :, 0:1] == slot, lanes % 16 < meta_ref[1, :, 0:1]
        )
        owner = jnp.sum(jnp.where(live, entry % rows + 1, 0), axis=0, keepdims=True) - 1
        pair = pl.ds(src_chip * 2, 2)

        for h in range(heads):
            keys = pool[pair, :, h * HEAD_SIZE : (h + 1) * HEAD_SIZE].reshape(span, HEAD_SIZE)
            vals = pool[pair, :, (heads + h) * HEAD_SIZE : (heads + h + 1) * HEAD_SIZE].reshape(
                span, HEAD_SIZE
            )
            k_scale = jnp.concatenate(
                [scales[src_chip * 2, h : h + 1, :], scales[src_chip * 2 + 1, h : h + 1, :]], axis=1
            ) * LOG2_SCALE
            v_scale = jnp.concatenate(
                [
                    scales[src_chip * 2, heads + h : heads + h + 1, :],
                    scales[src_chip * 2 + 1, heads + h : heads + h + 1, :],
                ],
                axis=1,
            )
            step = 128

            def body(t, _):
                rr = pl.ds(t * step, step)
                s = lax.dot_general(
                    qh[h, rr, :], keys, (((1,), (1,)), ((), ())), preferred_element_type=F32
                )
                req = lax.broadcasted_iota(jnp.int32, (step, span), 0) % rows
                s = jnp.where(req == owner, s * k_scale, -1e30)
                m_old = m_ref[h, rr, :]
                m_new = jnp.maximum(m_old, jnp.max(s, axis=1, keepdims=True))
                p = jnp.exp2(s - jnp.concatenate([m_new, m_new], axis=1))
                alpha = jnp.exp2(m_old - m_new)
                m_ref[h, rr, :] = m_new
                l_ref[h, rr, :] = alpha * l_ref[h, rr, :] + p[:, :tokens] + p[:, tokens:]
                mix = jnp.dot((p * v_scale).astype(BF16), vals, preferred_element_type=F32)
                acc[h, rr, :] = alpha * acc[h, rr, :] + mix
                return 0

            lax.fori_loop(0, group * rows // step, body, 0, unroll=True)

    for zz in range(depth):
        to_sibling(zz, 1 - y).start()
    for zz in range(depth):
        to_sibling(zz, y).start()
    attend_chip(0)
    for zz in range(depth):
        to_sibling(zz, 1 - y).wait_recv()
        there = at(zz, 1 - y, c)
        part[there] = (part[there].astype(F32) + r1[zz * 2 + 1 - y].astype(F32)).astype(BF16)
        to_y(zz).start()
    for zz in range(depth):
        to_sibling(zz, y).wait_recv()
        there = at(zz, y, c)
        part[there] = (part[there].astype(F32) + r1[zz * 2 + y].astype(F32)).astype(BF16)
    attend_chip(1)
    for d in range(1, depth + 1):
        zz = (z + d) % depth
        to_y(zz).wait_recv()
        there = at(zz, y, c)
        part[there] = (part[there].astype(F32) + r2[zz].astype(F32)).astype(BF16)
        if d < depth:
            to_z(d).start()
    for j in range(2, chips):
        attend_chip(j)
    total = part[me].astype(F32)
    for d in range(1, depth):
        to_z(d).wait_recv()
        total = total + r3[d - 1].astype(F32)
    moe_ref[...] = total.astype(BF16)

    for h in range(heads):
        for g in range(group):
            rr = slice(g * rows, (g + 1) * rows)
            at_lane = (h * group + g) * HEAD_SIZE
            norm = jnp.sum(l_ref[h, rr, :], axis=1, keepdims=True)
            attn_ref[:, at_lane : at_lane + HEAD_SIZE] = (acc[h, rr, :] / norm).astype(BF16)

    for zz in range(depth):

        @pl.when(jnp.logical_and(z < last, zz <= z))
        def _():
            ag_up(zz).wait_send()

        @pl.when(jnp.logical_and(z > 0, zz >= z))
        def _():
            ag_down(zz).wait_send()

        ag_y(zz).wait_send()
        for yy in range(2):
            ag_core(zz, yy).wait_send()
    for dest in kv_order:
        sc(dest, me).wait_send()
        kv(dest, me).wait_send()
    for zz in range(depth):
        for yy in range(2):
            to_sibling(zz, yy).wait_send()
        to_y(zz).wait_send()
    for d in range(1, depth):
        to_z(d).wait_send()


def fused_local(
    n,
    queries,
    incoming_key_value,
    key_value_codes,
    key_value_scales,
    lengths,
    block_table,
    hidden,
    routes,
    router,
    w_gate,
    w_up,
    w_down,
):
    rows, width = hidden.shape
    ff = w_gate.shape[2]
    blocks, block_tokens, features = key_value_codes.shape
    tokens = blocks // n * block_tokens
    depth = n // 4
    codes = key_value_codes.reshape(n, tokens, features)
    kinds = key_value_scales.shape[1]
    per_request = block_table.shape[2]
    q_rows = rows * QUERY_HEADS // KEY_VALUE_HEADS
    vmem = pl.BlockSpec(memory_space=pltpu.VMEM)
    hbm = pl.BlockSpec(memory_space=pltpu.HBM)
    dma = pltpu.SemaphoreType.DMA
    return pl.pallas_call(
        functools.partial(fused_kernel, n),
        out_shape=(
            jax.ShapeDtypeStruct(queries.shape, BF16),
            jax.ShapeDtypeStruct(hidden.shape, BF16),
        ),
        in_specs=[hbm] * 12,
        out_specs=(vmem, vmem),
        scratch_shapes=[
            pltpu.VMEM(queries.shape, BF16),
            pltpu.VMEM(incoming_key_value.shape, BF16),
            pltpu.VMEM((kinds, block_tokens, blocks), BF16),
            pltpu.VMEM((per_request, rows), jnp.int32),
            pltpu.VMEM((1, rows), jnp.int32),
            pltpu.VMEM((routes.shape[1], rows), jnp.int32),
            pltpu.VMEM((router.shape[1], width), BF16),
            pltpu.VMEM((n, 8, tokens), F32),
            pltpu.VMEM((2, per_request * rows, 128), jnp.int32),
            pltpu.VMEM((n, rows, width + 128), BF16),
            pltpu.VMEM((n, tokens, features), BF16),
            pltpu.VMEM((n, 8, tokens), F32),
            pltpu.VMEM((width, ff), BF16),
            pltpu.VMEM((width, ff), BF16),
            pltpu.VMEM((ff, width), BF16),
            pltpu.VMEM((n * rows, ff), BF16),
            pltpu.VMEM((n, rows, width), BF16),
            pltpu.VMEM((2 * depth, rows, width), BF16),
            pltpu.VMEM((depth, rows, width), BF16),
            pltpu.VMEM((depth - 1, rows, width), BF16),
            pltpu.VMEM((KEY_VALUE_HEADS, q_rows, HEAD_SIZE), BF16),
            pltpu.VMEM((KEY_VALUE_HEADS, q_rows, HEAD_SIZE), F32),
            pltpu.VMEM((KEY_VALUE_HEADS, q_rows, HEAD_SIZE), F32),
            pltpu.VMEM((KEY_VALUE_HEADS, q_rows, HEAD_SIZE), F32),
            dma((3,)),
            dma((1,)),
            dma((8,)),
            dma((2, depth)),
            dma((depth,)),
            dma((2 * depth,)),
            dma((n,)),
            dma((n,)),
            dma((n,)),
            dma((n,)),
            dma((n,)),
            dma((n - 1,)),
            dma((n - 1,)),
        ],
        compiler_params=pltpu.CompilerParams(
            collective_id=0, has_side_effects=True, vmem_limit_bytes=63 * 1024 * 1024
        ),
    )(
        queries,
        incoming_key_value,
        codes,
        jnp.transpose(key_value_scales, (1, 2, 0)),
        jnp.transpose(block_table[0]),
        lengths,
        hidden,
        jnp.transpose(routes),
        jnp.transpose(router),
        w_gate[0],
        w_up[0],
        w_down[0],
    )


def solution(mesh):
    in_specs = (
        P(("groups", "expert"), None),
        P(("groups", "expert"), None),
        P(("groups", "expert"), None, None),
        P(("groups", "expert"), None, None),
        P(("groups", "expert"), None),
        P(("groups", "expert"), None, None),
        P(("groups", "expert"), None),
        P(("groups", "expert"), None),
        P(),
        P("expert", None, None),
        P("expert", None, None),
        P("expert", None, None),
    )
    out_specs = (P(("groups", "expert"), None), P(("groups", "expert"), None))
    n = mesh.shape["expert"]
    body = functools.partial(fused_local, n) if n == 16 else local
    return jax.shard_map(body, mesh=mesh, in_specs=in_specs, out_specs=out_specs, check_vma=False)
```
